32 devices in a mesh: gx: 4 (over x, core), gy: 2 (over y), gz: 4 (over z).
Axes of the slice: x: 2, y: 2, z: 4, core: 2. Of those that a mesh axis runs over, the one named last changes fastest.
Arguments:
- features: bfloat16 [32, 8, 32, 512], P(None, 'gx', 'gy', 'gz'), may hold values from -6 to 6
- voxel_slot: int32 [8, 32, 512], P('gx', 'gy', 'gz'), may hold values from 0 to 1023
- conv_weight: bfloat16 [27, 32, 32], replicated, may hold values from -0.21875 to 0.21875
- conv_bias: float32 [32], replicated, may hold values from -3 to 3
- pair_owner: int32 [4096, 1], P(('gx', 'gy', 'gz')), may hold values from 0 to 7; in each aligned block of 128 rows (0 to 127, 128 to 255, ...) at most 40 rows name the same one
- pair_edge: int32 [4096], P(('gx', 'gy', 'gz')), may hold values from 0 to 63
- mlp_in: bfloat16 [256, 512], replicated, may hold values from -0.375 to 0.375
- mlp_in_bias: float32 [512], replicated, may hold values from -3 to 3
- mlp_mid: bfloat16 [512, 512], replicated, may hold values from -0.25 to 0.25
- mlp_mid_bias: float32 [512], replicated, may hold values from -3 to 3
- mlp_out: bfloat16 [512], replicated, may hold values from -0.25 to 0.25
Outputs:
- pair_scores: float32 [4096], P(('gx', 'gy', 'gz'))
The draws below stay inside these ranges and needn't reach their ends.
Inputs may be any that keep to these rules, and one draw needn't show every extreme that they name: `pair_owner`: within each aligned block of 128 rows (the pairs of one brick) no owner is named by more than 40 rows, a bound that some block reaches.
All inputs are finite; a program needn't handle non-finite values.
Results may differ from the reference program's by a relative error of at most 0.011.
Values may be sent and summed in bfloat16 or wider, within the bound.
A program may use at most 64 MiB of HBM per device.

```python
import math
import jax
import jax.numpy as jnp
import numpy as np
from jax import lax

C = 32
BINS = 8
HID = 512
BX = 2
BY = 16
BZ = 128
P_DEV = 128
EDGE_DEV = 64
ROW = 256
SLOTS = 1024
CAP = 40
NX = 8
NY = 32
NZ = 512
NPAIRS = 4096
N_GX = 4
N_GY = 2
N_GZ = 4


def place_ends(array, rng, smallest, top_value):
    index_at = [jax.random.randint(jax.random.fold_in(rng, axis), (), 0, length) for axis, length in enumerate(array.shape)]
    main_axis = array.shape.index(max(array.shape))
    beside = index_at[:main_axis] + [(index_at[main_axis] + 1) % array.shape[main_axis]] + index_at[main_axis + 1:]
    return array.at[tuple(index_at)].set(smallest).at[tuple(beside)].set(top_value)


def block_levels(stream_key, dims, shards, low, top_value):
    def one(position, parts):
        heights = jax.random.uniform(jax.random.fold_in(jax.random.fold_in(stream_key, 6), position), (parts,), jnp.float32, low / len(shards), top_value / len(shards))
        return jnp.repeat(jnp.exp(heights), dims[position] // parts).reshape((-1,) + (1,) * (len(dims) - position - 1))

    gain = one(*shards[0])
    for cut in shards[1:]:
        gain = gain * one(*cut)
    return gain


def routed_block(rng, own, number, rows, number_of, top, most, skew):
    sequence = jax.random.permutation(rng, number_of)
    crowded, usual = load_shares(number_of, rows * top, most, skew, True), load_shares(number_of, rows * top, most, skew, False)
    places = jnp.arange(number_of)

    def named(sizes, offset_by):
        used = int((sizes > 0).sum())
        fixed = max(1, used // 4)
        moved = fixed + (places - fixed + offset_by * (used - fixed)) % max(1, number_of - fixed)
        return jnp.zeros((number_of,), jnp.int32).at[sequence[jnp.where(places < fixed, places, moved)]].set(jnp.asarray(sizes, jnp.int32))

    sizes = jnp.where(number % 4 == 0, named(crowded, number // 4), named(usual, number - number // 4 - 1))
    mixed = jax.random.permutation(jax.random.fold_in(own, 3), number_of)
    giver, taker = mixed[0:number_of // 2 * 2:2], mixed[1:number_of // 2 * 2:2]
    room = jnp.minimum(sizes[giver] - 1, most - sizes[taker]) // 2
    room = jnp.where((giver == sequence[0]) | (taker == sequence[0]) | (sizes[taker] == 0), 0, jnp.maximum(room, 0))
    moved = jax.random.randint(jax.random.fold_in(own, 4), (number_of // 2,), 0, 1 << 20) % (room + 1)
    sizes = sizes.at[giver].add(-moved).at[taker].add(moved)
    items = jnp.searchsorted(jnp.cumsum(sizes), jnp.arange(rows * top), side="right").astype(jnp.int32)
    grid = items.reshape(top, rows).T
    grid = grid[jax.random.permutation(jax.random.fold_in(own, 1), rows)]
    offset_by = jax.random.randint(jax.random.fold_in(own, 2), (rows, 1), 0, top)
    return jnp.take_along_axis(grid, (jnp.arange(top)[None, :] + offset_by) % top, axis=1)


def load_shares(number_of, total, bound, lean, full):
    weights = [(1 << 20) // math.isqrt(standing ** lean) + 1 for standing in range(1, number_of + 1)]
    largest = bound if full else min(bound, max(-(-total // number_of), total * weights[0] // sum(weights)))
    least = 1 if total - largest >= number_of - 1 else 0
    holding, spare = [largest] + [least] * (number_of - 1), total - largest - least * (number_of - 1)
    while spare > 0:
        free = [i for i in range(1, number_of) if holding[i] < largest] or [i for i in range(1, number_of) if holding[i] < bound]
        pool, budget = sum([weights[i] for i in free]), spare
        for i in free:
            more = min(bound - holding[i], max(1, budget * weights[i] // pool), spare)
            holding[i] = holding[i] + more
            spare = spare - more
    return np.array(holding)


def centred(rng, dims, deviation, most, shards=(), kind=jnp.bfloat16):
    gain = block_levels(rng, dims, shards, -0.22, 0.18) if shards else 1.0
    result = jax.random.normal(rng, dims, jnp.float32) * deviation * gain
    return jnp.minimum(jnp.maximum(result, -most), most).astype(kind)


def setup_inputs(seed: int = 0) -> dict:
    streams_of = jax.random.split(jax.random.key(seed), 12)
    features = centred(streams_of[0], (C, NX, NY, NZ), 1.0, 6.0, ((1, 4), (2, 2), (3, 4)))
    voxel_slot = place_ends(jax.random.randint(streams_of[1], (NX, NY, NZ), 0, SLOTS), jax.random.fold_in(streams_of[1], 1), 0, SLOTS - 1).astype(jnp.int32)
    conv_weight = centred(streams_of[2], (27, C, C), (27 * C) ** -0.5, 0.21875)
    conv_bias = centred(streams_of[3], (C,), 0.5, 3.0, (), jnp.float32)
    pair_owner_keys = jax.random.split(jax.random.fold_in(streams_of[4], 1), NPAIRS // P_DEV)
    pair_owner_turns = jax.random.permutation(jax.random.fold_in(streams_of[4], 3), NPAIRS // P_DEV)
    pair_owner = jax.vmap(lambda own, number: routed_block(jax.random.fold_in(streams_of[4], 2), own, number, P_DEV, N_GX * N_GY, 1, CAP, 2))(pair_owner_keys, pair_owner_turns).reshape((NPAIRS, 1))
    pair_edge = place_ends(jax.random.randint(streams_of[5], (NPAIRS,), 0, EDGE_DEV), jax.random.fold_in(streams_of[5], 1), 0, EDGE_DEV - 1).astype(jnp.int32)
    mlp_in = centred(streams_of[6], (ROW, HID), ROW ** -0.5, 0.375)
    mlp_in_bias = centred(streams_of[7], (HID,), 0.5, 3.0, (), jnp.float32)
    mlp_mid = centred(streams_of[8], (HID, HID), HID ** -0.5, 0.25)
    mlp_mid_bias = centred(streams_of[9], (HID,), 0.5, 3.0, (), jnp.float32)
    mlp_out = centred(streams_of[10], (HID,), HID ** -0.5, 0.25)
    return {"features": features, "voxel_slot": voxel_slot, "conv_weight": conv_weight, "conv_bias": conv_bias, "pair_owner": pair_owner, "pair_edge": pair_edge, "mlp_in": mlp_in, "mlp_in_bias": mlp_in_bias, "mlp_mid": mlp_mid, "mlp_mid_bias": mlp_mid_bias, "mlp_out": mlp_out}


def reference(features, voxel_slot, conv_weight, conv_bias, pair_owner, pair_edge, mlp_in, mlp_in_bias, mlp_mid, mlp_mid_bias, mlp_out):
    volume_in = features.astype(jnp.float32)[None]
    kernel = conv_weight.astype(jnp.float32).reshape(3, 3, 3, C, C).transpose(3, 4, 0, 1, 2)
    conv_out = lax.conv_general_dilated(volume_in, kernel, (1, 1, 1), "SAME", precision=lax.Precision.HIGHEST)[0]
    fields = jnp.maximum(conv_out + conv_bias[:, None, None, None], 0.0).astype(jnp.bfloat16)
    bricks = N_GX * N_GY * N_GZ
    voxels = BX * BY * BZ
    brick_fields = fields.reshape(C, N_GX, BX, N_GY, BY, N_GZ, BZ).transpose(1, 3, 5, 2, 4, 6, 0).reshape(bricks * voxels, C)
    brick_slots = voxel_slot.reshape(N_GX, BX, N_GY, BY, N_GZ, BZ).transpose(0, 2, 4, 1, 3, 5).reshape(bricks, voxels)
    segment_ids = (brick_slots + (jnp.arange(bricks, dtype=jnp.int32) * SLOTS)[:, None]).reshape(-1)
    pooled = jax.ops.segment_sum(brick_fields.astype(jnp.float32), segment_ids, num_segments=bricks * SLOTS)
    pooled = pooled * (SLOTS / voxels)
    pair_rows = pooled.reshape(bricks, BINS, P_DEV, C).transpose(0, 2, 1, 3).reshape(NPAIRS, ROW).astype(jnp.bfloat16)
    brick_of_pair = jnp.arange(NPAIRS, dtype=jnp.int32) // P_DEV
    plane = brick_of_pair % N_GZ
    edge_ids = ((plane * (N_GX * N_GY) + pair_owner[:, 0]) * EDGE_DEV + pair_edge).astype(jnp.int32)
    edge_total = N_GZ * N_GX * N_GY * EDGE_DEV
    edge_rows = jax.ops.segment_sum(pair_rows.astype(jnp.float32), edge_ids, num_segments=edge_total).astype(jnp.bfloat16)
    first = jax.nn.silu(jnp.dot(edge_rows, mlp_in, preferred_element_type=jnp.float32) + mlp_in_bias).astype(jnp.bfloat16)
    second = jax.nn.silu(jnp.dot(first, mlp_mid, preferred_element_type=jnp.float32) + mlp_mid_bias).astype(jnp.bfloat16)
    edge_scores = jnp.dot(second, mlp_out, preferred_element_type=jnp.float32)
    return edge_scores[edge_ids]
```

```python
import jax
import jax.numpy as jnp
from jax import lax
from jax.sharding import PartitionSpec as P

BINS = 8
EDGE_DEV = 64


def extended(cells, sides, width):
    for axis, dim in sides:
        count = lax.axis_size(axis)
        ends = count - 1
        head = lax.slice_in_dim(cells, 0, width, axis=dim)
        tail = lax.slice_in_dim(cells, cells.shape[dim] - width, cells.shape[dim], axis=dim)
        cells = jnp.concatenate(
            [
                lax.ppermute(tail, axis, [(i, (i + 1) % count) for i in range(ends)]),
                cells,
                lax.ppermute(head, axis, [((i + 1) % count, i) for i in range(ends)]),
            ],
            axis=dim,
        )
    return cells


def body(
    features,
    voxel_slot,
    conv_weight,
    conv_bias,
    pair_owner,
    pair_edge,
    mlp_in,
    mlp_in_bias,
    mlp_mid,
    mlp_mid_bias,
    mlp_out,
):
    channels, extent_x, extent_y, extent_z = features.shape
    volume = extent_x * extent_y * extent_z
    padded = extended(features, (("gx", 1), ("gy", 2), ("gz", 3)), 1)
    total = jnp.zeros((channels, volume), jnp.float32)
    for offset in range(27):
        shift_x = offset // 9
        shift_y = offset // 3 % 3
        shift_z = offset % 3
        window = padded[
            :,
            shift_x : shift_x + extent_x,
            shift_y : shift_y + extent_y,
            shift_z : shift_z + extent_z,
        ].reshape(channels, volume)
        total = total + jnp.dot(conv_weight[offset], window, preferred_element_type=jnp.float32)
    fields = jnp.maximum(total + conv_bias[:, None], 0.0).astype(jnp.bfloat16)
    pair_count = pair_edge.shape[0]
    slot_count = pair_count * BINS
    slots_flat = voxel_slot.reshape(volume)
    block_width = 512
    pieces = []
    for block in range(slot_count // block_width):
        labels = block * block_width + lax.iota(jnp.int32, block_width)
        onehot = (slots_flat[:, None] == labels[None, :]).astype(jnp.bfloat16)
        pieces.append(jnp.dot(fields, onehot, preferred_element_type=jnp.float32))
    pooled = jnp.concatenate(pieces, axis=1) * (slot_count / volume)
    row_width = BINS * channels
    pair_rows = (
        pooled.reshape(channels, BINS, pair_count)
        .transpose(2, 1, 0)
        .reshape(pair_count, row_width)
        .astype(jnp.bfloat16)
    )
    size_gx = lax.axis_size("gx")
    size_gy = lax.axis_size("gy")
    groups = size_gx * size_gy
    capacity = max(2, (5 * pair_count + 2 * groups - 1) // (2 * groups))
    owners = pair_owner[:, 0]
    owner_marks = (owners[:, None] == lax.iota(jnp.int32, groups)[None, :]).astype(jnp.bfloat16)
    rows_at = lax.iota(jnp.int32, pair_count)
    before = (rows_at[None, :] < rows_at[:, None]).astype(jnp.bfloat16)
    earlier = jnp.dot(before, owner_marks, preferred_element_type=jnp.float32)
    slot_rank = jnp.sum(earlier * owner_marks, axis=1).astype(jnp.int32)
    target = owners * capacity + slot_rank
    placing = lax.iota(jnp.int32, groups * capacity)[:, None] == target[None, :]
    send_rows = jnp.dot(
        placing.astype(jnp.bfloat16), pair_rows, preferred_element_type=jnp.float32
    ).astype(jnp.bfloat16)
    send_ids = jnp.max(jnp.where(placing, pair_edge[None, :], -1), axis=1)
    edge_count = EDGE_DEV
    recv_rows, recv_ids = (
        lax.all_to_all(
            send_rows.reshape(groups, capacity, row_width),
            ("gx", "gy"),
            split_axis=0,
            concat_axis=0,
            tiled=True,
        ),
        lax.all_to_all(
            send_ids.reshape(groups, capacity),
            ("gx", "gy"),
            split_axis=0,
            concat_axis=0,
            tiled=True,
        ),
    )
    flat_rows = recv_rows.reshape(groups * capacity, row_width)
    flat_ids = recv_ids.reshape(groups * capacity)
    edge_onehot = (lax.iota(jnp.int32, edge_count)[:, None] == flat_ids[None, :]).astype(
        jnp.bfloat16
    )
    edge_rows = jnp.dot(edge_onehot, flat_rows, preferred_element_type=jnp.float32).astype(
        jnp.bfloat16
    )
    first = jax.nn.silu(
        jnp.dot(edge_rows, mlp_in, preferred_element_type=jnp.float32) + mlp_in_bias
    ).astype(jnp.bfloat16)
    second = jax.nn.silu(
        jnp.dot(first, mlp_mid, preferred_element_type=jnp.float32) + mlp_mid_bias
    ).astype(jnp.bfloat16)
    edge_scores = jnp.dot(second, mlp_out, preferred_element_type=jnp.float32)
    owner_scores = jnp.sum(
        jnp.where(
            lax.iota(jnp.int32, edge_count)[:, None] == flat_ids[None, :], edge_scores[:, None], 0.0
        ),
        axis=0,
    ).reshape(groups, capacity)
    returned = lax.all_to_all(owner_scores, ("gx", "gy"), split_axis=0, concat_axis=0, tiled=True)
    return jnp.sum(jnp.where(placing, returned.reshape(groups * capacity)[:, None], 0.0), axis=0)


def solution(mesh):
    placed = (
        P(None, "gx", "gy", "gz"),
        P("gx", "gy", "gz"),
        P(),
        P(),
        P(("gx", "gy", "gz"), None),
        P(("gx", "gy", "gz")),
        P(),
        P(),
        P(),
        P(),
        P(),
    )
    return jax.shard_map(
        body, mesh=mesh, in_specs=placed, out_specs=P(("gx", "gy", "gz")), check_vma=False
    )
```

```python
import functools

import jax
import jax.numpy as jnp
from jax import lax
from jax.experimental import pallas as pl
from jax.experimental.pallas import tpu as pltpu
from jax.sharding import PartitionSpec as P

BINS = 8
EDGE_DEV = 64
LANES = 128
BF = jnp.bfloat16
F32 = jnp.float32
MESH = pl.DeviceIdType.MESH
SIDES = [(sx, sy) for sx in (-1, 0, 1) for sy in (-1, 0, 1) if (sx, sy) != (0, 0)]
NT = (((1,), (1,)), ((), ()))


def iota(shape, axis):
    return lax.broadcasted_iota(jnp.int32, shape, axis)


def kernel(
    size_gx,
    size_gy,
    size_gz,
    capacity,
    block_rows,
    feat,
    slot,
    weight,
    bias,
    owner,
    edge,
    w_in_hbm,
    b_in,
    w_mid_hbm,
    b_mid,
    w_out,
    out,
    plain,
    ext,
    taps,
    pick,
    conv,
    bins_at,
    pooled,
    z_send,
    z_left,
    z_right,
    rows_send,
    rows_recv,
    ids_send,
    ids_recv,
    scores,
    scores_recv,
    w_in,
    w_mid,
    w_sem,
    xy_ssem,
    xy_rsem,
    z_ssem,
    z_rsem,
    row_ssem,
    row_rsem,
    id_ssem,
    id_rsem,
    sc_ssem,
    sc_rsem,
):
    groups = size_gx * size_gy
    channels, bx, by, bz = feat.shape
    gx, gy, gz = lax.axis_index("gx"), lax.axis_index("gy"), lax.axis_index("gz")
    me = gx * size_gy + gy
    pairs = by // 2

    in_copy = pltpu.make_async_copy(w_in_hbm, w_in, w_sem.at[0])
    mid_copy = pltpu.make_async_copy(w_mid_hbm, w_mid, w_sem.at[1])
    in_copy.start()
    mid_copy.start()

    ext[0] = jnp.zeros(ext.shape[1:], BF)
    ext[bx + 1] = jnp.zeros(ext.shape[1:], BF)
    for x in range(bx):
        ext[x + 1, 0] = jnp.zeros(ext.shape[2:], BF)
        ext[x + 1, by + 1] = jnp.zeros(ext.shape[2:], BF)
    z_left[...] = jnp.zeros_like(z_left)
    z_right[...] = jnp.zeros_like(z_right)
    rows_recv[...] = jnp.zeros_like(rows_recv)

    peers = [lax.rem(me + k, groups) for k in range(groups)]
    peer_ids = [{"gx": p // size_gy, "gy": lax.rem(p, size_gy)} for p in peers]
    has_left, has_right = gz > 0, gz < size_gz - 1
    barrier = pltpu.get_barrier_semaphore()
    for k in range(1, groups):
        pl.semaphore_signal(barrier, inc=1, device_id=peer_ids[k], device_id_type=MESH)

    @pl.when(has_left)
    def _():
        pl.semaphore_signal(barrier, inc=1, device_id={"gz": gz - 1}, device_id_type=MESH)

    @pl.when(has_right)
    def _():
        pl.semaphore_signal(barrier, inc=1, device_id={"gz": gz + 1}, device_id_type=MESH)

    plain[...] = feat[...].astype(F32).reshape(plain.shape)
    for x in range(bx):
        for y in range(by):
            part = plain[pl.ds(x * by + y, channels, stride=bx * by), :]
            ext[x + 1, y + 1] = part.astype(BF)

    greeted = groups - 1 + jnp.minimum(gz, 1) + jnp.minimum(size_gz - 1 - gz, 1)
    pl.semaphore_wait(barrier, greeted)

    def span(side, length):
        if side == 0:
            return pl.ds(1, length), pl.ds(1, length)
        return (pl.ds(length, 1), pl.ds(0, 1)) if side > 0 else (pl.ds(1, 1), pl.ds(length + 1, 1))

    def exists(sx, sy):
        x, y = gx + sx, gy + sy
        return (x >= 0) & (x < size_gx) & (y >= 0) & (y < size_gy)

    xy_copies = []
    for i, (sx, sy) in enumerate(SIDES):
        (x_from, x_to), (y_from, y_to) = span(sx, bx), span(sy, by)
        xy_copies.append(
            pltpu.make_async_remote_copy(
                src_ref=ext.at[x_from, y_from],
                dst_ref=ext.at[x_to, y_to],
                send_sem=xy_ssem.at[i],
                recv_sem=xy_rsem.at[i],
                device_id={"gx": gx + sx, "gy": gy + sy},
                device_id_type=MESH,
            )
        )
        pl.when(exists(sx, sy))(xy_copies[i].start)

    owner_row = owner[...]
    edge_row = edge[...]
    marks = iota((groups, LANES), 0) == owner_row
    marks_f = marks.astype(F32)
    before = (iota((LANES, LANES), 0) < iota((LANES, LANES), 1)).astype(BF)
    earlier = jnp.dot(marks_f.astype(BF), before, preferred_element_type=F32)
    rank = jnp.sum(earlier * marks_f, axis=0, keepdims=True).astype(jnp.int32)
    row_at = iota((LANES, LANES), 0)
    slot_marks = ((row_at == rank) | (row_at == rank + capacity)).astype(F32).astype(BF)
    numbered = jnp.where(marks, (edge_row + 1).astype(F32), 0.0).astype(BF)
    ids = lax.dot_general(numbered, slot_marks, NT, preferred_element_type=F32)
    ids = ids.astype(jnp.int32) - 1
    for g in range(groups):
        ids_send[g] = jnp.broadcast_to(ids[g : g + 1], (8, LANES))
    id_copies, row_copies, score_copies = [], [], []
    for k in range(1, groups):
        id_copies.append(
            pltpu.make_async_remote_copy(
                src_ref=ids_send.at[peers[k]],
                dst_ref=ids_recv.at[me],
                send_sem=id_ssem.at[k],
                recv_sem=id_rsem.at[k],
                device_id=peer_ids[k],
                device_id_type=MESH,
            )
        )
        row_copies.append(
            pltpu.make_async_remote_copy(
                src_ref=rows_send.at[peers[k]],
                dst_ref=rows_recv.at[me, pl.ds(0, block_rows)],
                send_sem=row_ssem.at[k],
                recv_sem=row_rsem.at[k],
                device_id=peer_ids[k],
                device_id_type=MESH,
            )
        )
        score_copies.append(
            pltpu.make_async_remote_copy(
                src_ref=scores,
                dst_ref=scores_recv.at[me],
                send_sem=sc_ssem.at[k],
                recv_sem=sc_rsem.at[k],
                device_id=peer_ids[k],
                device_id_type=MESH,
            )
        )
    for copy in id_copies:
        copy.start()
    ids_recv[me] = ids_send[me]

    width = 4 * channels
    spread = (
        (iota((channels, 4 * width), 1) // width * channels + iota((channels, 4 * width), 0))
        == iota((channels, 4 * width), 1) % width
    )
    placed = jnp.dot(
        weight[...].reshape(27 * channels, channels),
        spread.astype(F32).astype(BF),
        preferred_element_type=F32,
    )
    taps[...] = jnp.zeros_like(taps)
    for dz in range(3):
        for dx in range(3):
            for y in range(2):
                block = None
                for dy in range(3):
                    tap = 9 * dx + 3 * dy + dz
                    term = placed[
                        tap * channels : (tap + 1) * channels, (y + dy) * width : (y + dy + 1) * width
                    ]
                    block = term if block is None else block + term
                block = block.astype(BF)
                for x in range(2):
                    row = ((dz * 2 + x) * 2 + y) * channels
                    taps[row : row + channels, (x + dx) * width : (x + dx + 1) * width] = block

    tall = (by + 2) * bz
    at_y, at_z, lane = iota((tall, LANES), 0) // bz, iota((tall, LANES), 0) % bz, iota((tall, LANES), 1)
    pick[...] = (
        ((at_z == bz - 1) & (lane == at_y)) | ((at_z == 0) & (lane == at_y + 64))
    ).astype(F32).astype(BF)

    def mark_bins(j, carry):
        for part in range(4):
            x, y = part // 2, part % 2
            line = slot[pl.ds(x * by + 2 * j + y, 1), :] & (LANES - 1)
            hot = iota((LANES, bz), 0) == line
            bins_at[j, :, part * bz : (part + 1) * bz] = hot.astype(F32).astype(BF)
        return carry

    lax.fori_loop(0, pairs, mark_bins, 0)

    for i, (sx, sy) in enumerate(SIDES):
        pl.when(exists(-sx, -sy))(xy_copies[i].wait_recv)

    cut = jnp.concatenate(
        [ext[:, y].reshape((bx + 2) * channels, bz) for y in range(by + 2)], axis=1
    )
    z_send[...] = jnp.dot(cut, pick[...], preferred_element_type=F32).astype(BF)
    to_right = pltpu.make_async_remote_copy(
        src_ref=z_send,
        dst_ref=z_left,
        send_sem=z_ssem.at[0],
        recv_sem=z_rsem.at[0],
        device_id={"gz": gz + 1},
        device_id_type=MESH,
    )
    to_left = pltpu.make_async_remote_copy(
        src_ref=z_send,
        dst_ref=z_right,
        send_sem=z_ssem.at[1],
        recv_sem=z_rsem.at[1],
        device_id={"gz": gz - 1},
        device_id_type=MESH,
    )
    pl.when(has_right)(to_right.start)
    pl.when(has_left)(to_left.start)

    def convolve(i, carry):
        window = jnp.concatenate(
            [
                ext[:, pl.ds(4 * i + 2 * half, 4)].reshape((bx + 2) * 4 * channels, bz)
                for half in range(2)
            ],
            axis=1,
        )
        result = jnp.dot(taps[...], window, preferred_element_type=F32)
        conv[2 * i] = result[:, :bz]
        conv[2 * i + 1] = result[:, bz:]
        return carry

    lax.fori_loop(0, pairs // 2, convolve, 0)

    pl.when(has_left)(to_right.wait_recv)
    pl.when(has_right)(to_left.wait_recv)
    zlane = iota(z_left.shape, 1)
    faces = jnp.where(zlane < 64, z_left[...].astype(F32), z_right[...].astype(F32))
    moved = [faces] + [pltpu.roll(faces, LANES - y, 1) for y in range(1, 4)]
    window = jnp.concatenate(
        [
            moved[y][x * channels : (x + 1) * channels]
            for x in range(bx + 2)
            for y in range(4)
        ],
        axis=0,
    ).astype(BF)
    ends = jnp.dot(taps[...], window, preferred_element_type=F32)
    mrows = 4 * channels

    pooled[...] = jnp.zeros_like(pooled)
    lane32 = iota((channels, bz), 1)
    bias_col = bias[...]

    def pool(j, carry):
        wide = []
        for part in range(4):
            x, y = part // 2, part % 2
            row = part * channels
            base = (x * 2) * channels
            height = 2 * j + y
            low = pltpu.roll(ends[base : base + channels], LANES - height, 1)
            high = pltpu.roll(ends[2 * mrows + base : 2 * mrows + base + channels], 63 - height, 1)
            lower = pltpu.roll(conv[j, row : row + channels], 1, 1)
            upper = pltpu.roll(conv[j, 2 * mrows + row : 2 * mrows + row + channels], bz - 1, 1)
            total = conv[j, mrows + row : mrows + row + channels]
            total = total + jnp.where(lane32 == 0, low, lower)
            total = total + jnp.where(lane32 == bz - 1, high, upper)
            field = jnp.maximum(total + bias_col, 0.0)
            bin_row = slot[pl.ds(x * by + height, 1), :] // LANES
            wide.append(
                jnp.concatenate(
                    [jnp.where(bin_row == b, field, 0.0) for b in range(BINS)], axis=0
                ).astype(BF)
            )
        pooled[...] += lax.dot_general(
            bins_at[j], jnp.concatenate(wide, axis=1), NT, preferred_element_type=F32
        )
        return carry

    lax.fori_loop(0, pairs, pool, 0)
    share = (LANES * BINS) / (bx * by * bz)
    rows = (pooled[...] * share).astype(BF)

    target = owner_row * block_rows + rank
    at = iota((groups * block_rows, LANES), 0)
    sent = jnp.dot(
        (at == target).astype(F32).astype(BF), rows[:, :LANES], preferred_element_type=F32
    ) + jnp.dot(
        (at == target + capacity).astype(F32).astype(BF), rows[:, LANES:], preferred_element_type=F32
    )
    rows_send[...] = sent.astype(BF).reshape(rows_send.shape)
    for copy in row_copies:
        copy.start()
    rows_recv[me, 0:block_rows] = rows_send[me]

    for copy in id_copies:
        copy.wait_recv()
    at_lane = iota((EDGE_DEV, LANES), 1)
    at_edge = iota((EDGE_DEV, LANES), 0)
    first_half, second_half = [], []
    for g in range(groups):
        named = ids_recv[g][0:1] == at_edge
        first_half.append((named & (at_lane < capacity)).astype(F32).astype(BF))
        second_half.append(
            (named & (at_lane >= capacity) & (at_lane < 2 * capacity)).astype(F32).astype(BF)
        )
    first_half = jnp.concatenate(first_half, axis=1)
    second_half = jnp.concatenate(second_half, axis=1)
    in_copy.wait()
    mid_copy.wait()
    for copy in row_copies:
        copy.wait_recv()
    arrived = rows_recv[...].reshape(groups * LANES, LANES)
    edge_rows = jnp.concatenate(
        [
            jnp.dot(first_half, arrived, preferred_element_type=F32),
            jnp.dot(second_half, arrived, preferred_element_type=F32),
        ],
        axis=1,
    ).astype(BF)

    def silu(v):
        return v / (1.0 + jnp.exp(-v))

    first = silu(jnp.dot(edge_rows, w_in[...], preferred_element_type=F32) + b_in[...]).astype(BF)
    second = silu(jnp.dot(first, w_mid[...], preferred_element_type=F32) + b_mid[...]).astype(BF)
    last = jnp.broadcast_to(w_out[...].astype(F32), (16, w_out.shape[1])).astype(BF)
    final = lax.dot_general(last, second, NT, preferred_element_type=F32)
    scores[...] = jnp.concatenate([final[:8], final[8:]], axis=1)
    for copy in score_copies:
        copy.start()
    scores_recv[me] = scores[...]
    edge_hot = (iota((LANES, LANES), 0) == edge_row).astype(F32)
    for copy in score_copies:
        copy.wait_recv()
    table = jnp.concatenate([scores_recv[g][0:1] for g in range(groups)], axis=0)
    chosen = jnp.dot(table, edge_hot, preferred_element_type=F32, precision=lax.Precision.HIGHEST)
    out[...] = jnp.sum(jnp.where(marks, chosen, 0.0), axis=0, keepdims=True)

    for i, (sx, sy) in enumerate(SIDES):
        pl.when(exists(sx, sy))(xy_copies[i].wait_send)
    pl.when(has_right)(to_right.wait_send)
    pl.when(has_left)(to_left.wait_send)
    for copy in id_copies + row_copies + score_copies:
        copy.wait_send()


def body(
    features,
    voxel_slot,
    conv_weight,
    conv_bias,
    pair_owner,
    pair_edge,
    mlp_in,
    mlp_in_bias,
    mlp_mid,
    mlp_mid_bias,
    mlp_out,
):
    channels, bx, by, bz = features.shape
    sizes = [lax.axis_size(axis) for axis in ("gx", "gy", "gz")]
    groups = sizes[0] * sizes[1]
    pair_count = pair_edge.shape[0]
    capacity = max(2, (5 * pair_count + 2 * groups - 1) // (2 * groups))
    block_rows = -(-2 * capacity // 16) * 16
    hidden = mlp_mid.shape[0]
    vmem = pl.BlockSpec(memory_space=pltpu.VMEM)
    hbm = pl.BlockSpec(memory_space=pl.ANY)
    sems = pltpu.SemaphoreType.DMA
    result = pl.pallas_call(
        functools.partial(kernel, *sizes, capacity, block_rows),
        out_shape=jax.ShapeDtypeStruct((1, pair_count), F32),
        in_specs=[vmem] * 6 + [hbm, vmem, hbm, vmem, vmem],
        out_specs=vmem,
        scratch_shapes=[
            pltpu.VMEM((channels * bx * by, bz), F32),
            pltpu.VMEM((bx + 2, by + 2, channels, bz), BF),
            pltpu.VMEM((12 * channels, 16 * channels), BF),
            pltpu.VMEM(((by + 2) * bz, LANES), BF),
            pltpu.VMEM((by // 2, 12 * channels, bz), F32),
            pltpu.VMEM((by // 2, LANES, 4 * bz), BF),
            pltpu.VMEM((pair_count, BINS * channels), F32),
            pltpu.VMEM(((bx + 2) * channels, LANES), BF),
            pltpu.VMEM(((bx + 2) * channels, LANES), BF),
            pltpu.VMEM(((bx + 2) * channels, LANES), BF),
            pltpu.VMEM((groups, block_rows, LANES), BF),
            pltpu.VMEM((groups, LANES, LANES), BF),
            pltpu.VMEM((groups, 8, LANES), jnp.int32),
            pltpu.VMEM((groups, 8, LANES), jnp.int32),
            pltpu.VMEM((8, LANES), F32),
            pltpu.VMEM((groups, 8, LANES), F32),
            pltpu.VMEM(mlp_in.shape, BF),
            pltpu.VMEM(mlp_mid.shape, BF),
            sems((2,)),
            sems((8,)),
            sems((8,)),
            sems((2,)),
            sems((2,)),
            sems((groups,)),
            sems((groups,)),
            sems((groups,)),
            sems((groups,)),
            sems((groups,)),
            sems((groups,)),
        ],
        compiler_params=pltpu.CompilerParams(
            collective_id=0, has_side_effects=True, vmem_limit_bytes=40 * 2**20
        ),
    )(
        features,
        voxel_slot.reshape(bx * by, bz),
        conv_weight,
        conv_bias.reshape(channels, 1),
        pair_owner.reshape(1, pair_count),
        pair_edge.reshape(1, pair_count),
        mlp_in,
        mlp_in_bias.reshape(1, hidden),
        mlp_mid,
        mlp_mid_bias.reshape(1, hidden),
        mlp_out.reshape(1, hidden),
    )
    return result.reshape(pair_count)


def solution(mesh):
    placed = (
        P(None, "gx", "gy", "gz"),
        P("gx", "gy", "gz"),
        P(),
        P(),
        P(("gx", "gy", "gz"), None),
        P(("gx", "gy", "gz")),
        P(),
        P(),
        P(),
        P(),
        P(),
    )
    return jax.shard_map(
        body, mesh=mesh, in_specs=placed, out_specs=P(("gx", "gy", "gz")), check_vma=False
    )
```

```python
import functools

import jax
import jax.numpy as jnp
from jax import lax
from jax.experimental import pallas as pl
from jax.experimental.pallas import tpu as pltpu
from jax.sharding import PartitionSpec as P

BINS = 8
EDGE_DEV = 64
LANES = 128
BF = jnp.bfloat16
F32 = jnp.float32
MESH = pl.DeviceIdType.MESH
SIDES = [(sx, sy) for sx in (-1, 0, 1) for sy in (-1, 0, 1) if (sx, sy) != (0, 0)]
NT = (((1,), (1,)), ((), ()))


def iota(shape, axis):
    return lax.broadcasted_iota(jnp.int32, shape, axis)


def kernel(
    size_gx,
    size_gy,
    size_gz,
    capacity,
    block_rows,
    *refs,
):
    sources, out = refs[:11], refs[11]
    (feat, slot, weight, bias, owner, edge, w_in, b_in, w_mid, b_mid, w_out) = refs[12:23]
    (
        plain,
        ext,
        taps,
        pick,
        placing,
        conv,
        bins_at,
        pooled,
        z_send,
        z_left,
        z_right,
        rows_send,
        rows_recv,
        ids_send,
        ids_recv,
        scores,
        scores_recv,
        w_sem,
        xy_ssem,
        xy_rsem,
        z_ssem,
        z_rsem,
        row_ssem,
        row_rsem,
        id_ssem,
        id_rsem,
        sc_ssem,
        sc_rsem,
    ) = refs[23:]
    groups = size_gx * size_gy
    channels, bx, by, bz = feat.shape
    gx, gy, gz = lax.axis_index("gx"), lax.axis_index("gy"), lax.axis_index("gz")
    me = gx * size_gy + gy
    pairs = by // 2

    loads = [
        pltpu.make_async_copy(source, refs[12 + i], w_sem.at[i]) for i, source in enumerate(sources)
    ]
    for load in loads:
        load.start()

    ext[0] = jnp.zeros(ext.shape[1:], BF)
    ext[bx + 1] = jnp.zeros(ext.shape[1:], BF)
    for x in range(bx):
        ext[x + 1, 0] = jnp.zeros(ext.shape[2:], BF)
        ext[x + 1, by + 1] = jnp.zeros(ext.shape[2:], BF)
    z_left[...] = jnp.zeros_like(z_left)
    z_right[...] = jnp.zeros_like(z_right)
    if block_rows < LANES:
        spare = (groups, LANES - block_rows, LANES)
        rows_recv[:, block_rows:] = jnp.zeros(spare, BF)

    peers = [lax.rem(me + k, groups) for k in range(groups)]
    peer_ids = [{"gx": p // size_gy, "gy": lax.rem(p, size_gy)} for p in peers]
    has_left, has_right = gz > 0, gz < size_gz - 1
    barrier = pltpu.get_barrier_semaphore()
    for k in range(1, groups):
        pl.semaphore_signal(barrier, inc=1, device_id=peer_ids[k], device_id_type=MESH)

    @pl.when(has_left)
    def _():
        pl.semaphore_signal(barrier, inc=1, device_id={"gz": gz - 1}, device_id_type=MESH)

    @pl.when(has_right)
    def _():
        pl.semaphore_signal(barrier, inc=1, device_id={"gz": gz + 1}, device_id_type=MESH)

    loads[0].wait()
    plain[...] = feat[...].astype(F32).reshape(plain.shape)
    for x in range(bx):
        for y in range(by):
            part = plain[pl.ds(x * by + y, channels, stride=bx * by), :]
            ext[x + 1, y + 1] = part.astype(BF)

    greeted = groups - 1 + jnp.minimum(gz, 1) + jnp.minimum(size_gz - 1 - gz, 1)
    pl.semaphore_wait(barrier, greeted)

    def span(side, length):
        if side == 0:
            return pl.ds(1, length), pl.ds(1, length)
        return (pl.ds(length, 1), pl.ds(0, 1)) if side > 0 else (pl.ds(1, 1), pl.ds(length + 1, 1))

    def exists(sx, sy):
        x, y = gx + sx, gy + sy
        return (x >= 0) & (x < size_gx) & (y >= 0) & (y < size_gy)

    xy_copies = []
    for i, (sx, sy) in enumerate(SIDES):
        (x_from, x_to), (y_from, y_to) = span(sx, bx), span(sy, by)
        xy_copies.append(
            pltpu.make_async_remote_copy(
                src_ref=ext.at[x_from, y_from],
                dst_ref=ext.at[x_to, y_to],
                send_sem=xy_ssem.at[i],
                recv_sem=xy_rsem.at[i],
                device_id={"gx": gx + sx, "gy": gy + sy},
                device_id_type=MESH,
            )
        )
        pl.when(exists(sx, sy))(xy_copies[i].start)

    for load in loads[1:6]:
        load.wait()

    owner_row = owner[...]
    edge_row = edge[...]
    marks = iota((groups, LANES), 0) == owner_row
    marks_f = marks.astype(F32)
    before = (iota((LANES, LANES), 0) < iota((LANES, LANES), 1)).astype(BF)
    earlier = jnp.dot(marks_f.astype(BF), before, preferred_element_type=F32)
    rank = jnp.sum(earlier * marks_f, axis=0, keepdims=True).astype(jnp.int32)
    row_at = iota((LANES, LANES), 0)
    slot_marks = ((row_at == rank) | (row_at == rank + capacity)).astype(F32).astype(BF)
    numbered = jnp.where(marks, (edge_row + 1).astype(F32), 0.0).astype(BF)
    ids = lax.dot_general(numbered, slot_marks, NT, preferred_element_type=F32)
    ids = ids.astype(jnp.int32) - 1
    for g in range(groups):
        ids_send[g] = jnp.broadcast_to(ids[g : g + 1], (8, LANES))
    id_copies, row_copies, score_copies = [], [], []
    for k in range(1, groups):
        id_copies.append(
            pltpu.make_async_remote_copy(
                src_ref=ids_send.at[peers[k]],
                dst_ref=ids_recv.at[me],
                send_sem=id_ssem.at[k],
                recv_sem=id_rsem.at[k],
                device_id=peer_ids[k],
                device_id_type=MESH,
            )
        )
        row_copies.append(
            pltpu.make_async_remote_copy(
                src_ref=rows_send.at[peers[k]],
                dst_ref=rows_recv.at[me, pl.ds(0, block_rows)],
                send_sem=row_ssem.at[k],
                recv_sem=row_rsem.at[k],
                device_id=peer_ids[k],
                device_id_type=MESH,
            )
        )
        score_copies.append(
            pltpu.make_async_remote_copy(
                src_ref=scores,
                dst_ref=scores_recv.at[me],
                send_sem=sc_ssem.at[k],
                recv_sem=sc_rsem.at[k],
                device_id=peer_ids[k],
                device_id_type=MESH,
            )
        )
    for copy in id_copies:
        copy.start()
    ids_recv[me] = ids_send[me]

    width = 4 * channels
    spread = iota((channels, width), 1) == iota((channels, width), 0)
    placed = jnp.dot(
        weight[...].reshape(27 * channels, channels),
        spread.astype(F32).astype(BF),
        preferred_element_type=F32,
    )
    for x in range(2):
        for dz in range(3):
            row = (dz * 2 + x) * 2 * channels
            lost = 3 * (1 - x) * width
            taps[row : row + 2 * channels, lost : lost + width] = jnp.zeros((2 * channels, width), BF)
    for dz in range(3):
        for dx in range(3):
            block = None
            for dy in range(3):
                tap = 9 * dx + 3 * dy + dz
                term = placed[tap * channels : (tap + 1) * channels]
                term = pltpu.roll(term, dy * channels, 1) if dy else term
                block = term if block is None else block + term
            both = jnp.concatenate([block, pltpu.roll(block, channels, 1)], axis=0).astype(BF)
            for x in range(2):
                row = (dz * 2 + x) * 2 * channels
                taps[row : row + 2 * channels, (x + dx) * width : (x + dx + 1) * width] = both

    at_z, lane = iota((bz, LANES), 0), iota((bz, LANES), 1)
    last_z, first_z = at_z == bz - 1, at_z == 0
    for y in range(by + 2):
        chosen_z = (last_z & (lane == y)) | (first_z & (lane == y + 64))
        pick[y * bz : (y + 1) * bz] = chosen_z.astype(F32).astype(BF)

    target = owner_row * block_rows + rank
    block_at = iota((block_rows, LANES), 0)
    for g in range(groups):
        at = block_at + g * block_rows
        mine = owner_row == g
        placing[0, g * block_rows : (g + 1) * block_rows] = (
            ((at == target) & mine).astype(F32).astype(BF)
        )
        placing[1, g * block_rows : (g + 1) * block_rows] = (
            ((at == target + capacity) & mine).astype(F32).astype(BF)
        )

    def mark_bins(j, carry):
        for part in range(4):
            x, y = part // 2, part % 2
            line = slot[pl.ds(x * by + 2 * j + y, 1), :] & (LANES - 1)
            hot = iota((LANES, bz), 0) == line
            bins_at[j, :, part * bz : (part + 1) * bz] = hot.astype(F32).astype(BF)
        return carry

    lax.fori_loop(0, pairs, mark_bins, 0)

    for i, (sx, sy) in enumerate(SIDES):
        pl.when(exists(-sx, -sy))(xy_copies[i].wait_recv)

    cut = jnp.concatenate(
        [ext[:, y].reshape((bx + 2) * channels, bz) for y in range(by + 2)], axis=1
    )
    z_send[...] = jnp.dot(cut, pick[...], preferred_element_type=F32).astype(BF)
    to_right = pltpu.make_async_remote_copy(
        src_ref=z_send,
        dst_ref=z_left,
        send_sem=z_ssem.at[0],
        recv_sem=z_rsem.at[0],
        device_id={"gz": gz + 1},
        device_id_type=MESH,
    )
    to_left = pltpu.make_async_remote_copy(
        src_ref=z_send,
        dst_ref=z_right,
        send_sem=z_ssem.at[1],
        recv_sem=z_rsem.at[1],
        device_id={"gz": gz - 1},
        device_id_type=MESH,
    )
    pl.when(has_right)(to_right.start)
    pl.when(has_left)(to_left.start)

    def convolve(i, carry):
        window = jnp.concatenate(
            [
                ext[:, pl.ds(4 * i + 2 * half, 4)].reshape((bx + 2) * 4 * channels, bz)
                for half in range(2)
            ],
            axis=1,
        )
        result = jnp.dot(taps[...], window, preferred_element_type=F32)
        conv[2 * i] = result[:, :bz]
        conv[2 * i + 1] = result[:, bz:]
        return carry

    lax.fori_loop(0, pairs // 2, convolve, 0)

    pl.when(has_left)(to_right.wait_recv)
    pl.when(has_right)(to_left.wait_recv)
    zlane = iota(z_left.shape, 1)
    faces = jnp.where(zlane < 64, z_left[...].astype(F32), z_right[...].astype(F32))
    moved = [faces] + [pltpu.roll(faces, LANES - y, 1) for y in range(1, 4)]
    window = jnp.concatenate(
        [
            moved[y][x * channels : (x + 1) * channels]
            for x in range(bx + 2)
            for y in range(4)
        ],
        axis=0,
    ).astype(BF)
    ends = jnp.dot(taps[...], window, preferred_element_type=F32)
    mrows = 4 * channels

    pooled[...] = jnp.zeros_like(pooled)
    lane32 = iota((channels, bz), 1)
    own_channel = iota((channels, channels), 0) == iota((channels, channels), 1)
    bias_col = jnp.sum(jnp.where(own_channel, bias[...], 0.0), axis=1, keepdims=True)

    def pool(j, carry):
        wide = []
        for part in range(4):
            x, y = part // 2, part % 2
            row = part * channels
            base = (x * 2) * channels
            height = 2 * j + y
            low = pltpu.roll(ends[base : base + channels], LANES - height, 1)
            high = pltpu.roll(ends[2 * mrows + base : 2 * mrows + base + channels], 63 - height, 1)
            lower = pltpu.roll(conv[j, row : row + channels], 1, 1)
            upper = pltpu.roll(conv[j, 2 * mrows + row : 2 * mrows + row + channels], bz - 1, 1)
            total = conv[j, mrows + row : mrows + row + channels]
            total = total + jnp.where(lane32 == 0, low, lower)
            total = total + jnp.where(lane32 == bz - 1, high, upper)
            field = jnp.maximum(total + bias_col, 0.0)
            bin_row = slot[pl.ds(x * by + height, 1), :] >> 7
            wide.append(
                jnp.concatenate(
                    [jnp.where(bin_row == b, field, 0.0) for b in range(BINS)], axis=0
                ).astype(BF)
            )
        pooled[...] += lax.dot_general(
            bins_at[j], jnp.concatenate(wide, axis=1), NT, preferred_element_type=F32
        )
        return carry

    lax.fori_loop(0, pairs, pool, 0)
    share = (LANES * BINS) / (bx * by * bz)
    rows = (pooled[...] * share).astype(BF)

    sent = jnp.dot(placing[0], rows[:, :LANES], preferred_element_type=F32) + jnp.dot(
        placing[1], rows[:, LANES:], preferred_element_type=F32
    )
    rows_send[...] = sent.astype(BF).reshape(rows_send.shape)
    for copy in row_copies:
        copy.start()
    rows_recv[me, 0:block_rows] = rows_send[me]

    for copy in id_copies:
        copy.wait_recv()
    at_lane = iota((EDGE_DEV, LANES), 1)
    at_edge = iota((EDGE_DEV, LANES), 0)
    first_half, second_half = [], []
    for g in range(groups):
        named = ids_recv[g][0:1] == at_edge
        first_half.append((named & (at_lane < capacity)).astype(F32).astype(BF))
        second_half.append(
            (named & (at_lane >= capacity) & (at_lane < 2 * capacity)).astype(F32).astype(BF)
        )
    first_half = jnp.concatenate(first_half, axis=1)
    second_half = jnp.concatenate(second_half, axis=1)
    for load in loads[6:]:
        load.wait()
    for copy in row_copies:
        copy.wait_recv()
    arrived = rows_recv[...].reshape(groups * LANES, LANES)
    edge_rows = jnp.concatenate(
        [
            jnp.dot(first_half, arrived, preferred_element_type=F32),
            jnp.dot(second_half, arrived, preferred_element_type=F32),
        ],
        axis=1,
    ).astype(BF)

    def silu(v):
        return v / (1.0 + jnp.exp(-v))

    first = silu(jnp.dot(edge_rows, w_in[...], preferred_element_type=F32) + b_in[...]).astype(BF)
    second = silu(jnp.dot(first, w_mid[...], preferred_element_type=F32) + b_mid[...]).astype(BF)
    last = jnp.broadcast_to(w_out[...].astype(F32).reshape(1, -1), (16, w_out.shape[0])).astype(BF)
    final = lax.dot_general(last, second, NT, preferred_element_type=F32)
    scores[...] = jnp.concatenate([final[:8], final[8:]], axis=1)
    for copy in score_copies:
        copy.start()
    scores_recv[me] = scores[...]
    edge_hot = (iota((LANES, LANES), 0) == edge_row).astype(F32)
    for copy in score_copies:
        copy.wait_recv()
    table = jnp.concatenate([scores_recv[g][0:1] for g in range(groups)], axis=0)
    chosen = jnp.dot(table, edge_hot, preferred_element_type=F32, precision=lax.Precision.HIGHEST)
    out[...] = jnp.sum(jnp.where(marks, chosen, 0.0), axis=0, keepdims=True)

    for i, (sx, sy) in enumerate(SIDES):
        pl.when(exists(sx, sy))(xy_copies[i].wait_send)
    pl.when(has_right)(to_right.wait_send)
    pl.when(has_left)(to_left.wait_send)
    for copy in id_copies + row_copies + score_copies:
        copy.wait_send()


def body(
    features,
    voxel_slot,
    conv_weight,
    conv_bias,
    pair_owner,
    pair_edge,
    mlp_in,
    mlp_in_bias,
    mlp_mid,
    mlp_mid_bias,
    mlp_out,
):
    channels, bx, by, bz = features.shape
    sizes = [lax.axis_size(axis) for axis in ("gx", "gy", "gz")]
    groups = sizes[0] * sizes[1]
    pair_count = pair_edge.shape[0]
    capacity = max(2, (5 * pair_count + 2 * groups - 1) // (2 * groups))
    block_rows = -(-2 * capacity // 16) * 16
    hidden = mlp_mid.shape[0]
    vmem = pl.BlockSpec(memory_space=pltpu.VMEM)
    hbm = pl.BlockSpec(memory_space=pltpu.HBM)
    operands = (
        features,
        voxel_slot.reshape(bx * by, bz),
        conv_weight,
        conv_bias.reshape(1, channels),
        pair_owner.reshape(1, pair_count),
        pair_edge.reshape(1, pair_count),
        mlp_in,
        mlp_in_bias.reshape(1, hidden),
        mlp_mid,
        mlp_mid_bias.reshape(1, hidden),
        mlp_out,
    )
    sems = pltpu.SemaphoreType.DMA
    result = pl.pallas_call(
        functools.partial(kernel, *sizes, capacity, block_rows),
        out_shape=jax.ShapeDtypeStruct((1, pair_count), F32),
        in_specs=[hbm] * len(operands),
        out_specs=vmem,
        scratch_shapes=[pltpu.VMEM(a.shape, a.dtype) for a in operands]
        + [
            pltpu.VMEM((channels * bx * by, bz), F32),
            pltpu.VMEM((bx + 2, by + 2, channels, bz), BF),
            pltpu.VMEM((12 * channels, 16 * channels), BF),
            pltpu.VMEM(((by + 2) * bz, LANES), BF),
            pltpu.VMEM((2, groups * block_rows, LANES), BF),
            pltpu.VMEM((by // 2, 12 * channels, bz), F32),
            pltpu.VMEM((by // 2, LANES, 4 * bz), BF),
            pltpu.VMEM((pair_count, BINS * channels), F32),
            pltpu.VMEM(((bx + 2) * channels, LANES), BF),
            pltpu.VMEM(((bx + 2) * channels, LANES), BF),
            pltpu.VMEM(((bx + 2) * channels, LANES), BF),
            pltpu.VMEM((groups, block_rows, LANES), BF),
            pltpu.VMEM((groups, LANES, LANES), BF),
            pltpu.VMEM((groups, 8, LANES), jnp.int32),
            pltpu.VMEM((groups, 8, LANES), jnp.int32),
            pltpu.VMEM((8, LANES), F32),
            pltpu.VMEM((groups, 8, LANES), F32),
            sems((len(operands),)),
            sems((8,)),
            sems((8,)),
            sems((2,)),
            sems((2,)),
            sems((groups,)),
            sems((groups,)),
            sems((groups,)),
            sems((groups,)),
            sems((groups,)),
            sems((groups,)),
        ],
        compiler_params=pltpu.CompilerParams(
            collective_id=0, has_side_effects=True, vmem_limit_bytes=63 * 2**20
        ),
    )(*operands)
    return result.reshape(pair_count)


def solution(mesh):
    placed = (
        P(None, "gx", "gy", "gz"),
        P("gx", "gy", "gz"),
        P(),
        P(),
        P(("gx", "gy", "gz"), None),
        P(("gx", "gy", "gz")),
        P(),
        P(),
        P(),
        P(),
        P(),
    )
    return jax.shard_map(
        body, mesh=mesh, in_specs=placed, out_specs=P(("gx", "gy", "gz")), check_vma=False
    )
```

```python
import functools

import jax
import jax.numpy as jnp
from jax import lax
from jax.experimental import pallas as pl
from jax.experimental.pallas import tpu as pltpu
from jax.sharding import PartitionSpec as P

BINS = 8
EDGE_DEV = 64
LANES = 128
BF = jnp.bfloat16
F32 = jnp.float32
MESH = pl.DeviceIdType.MESH
SIDES = [(-1, 0), (1, 0), (0, -1), (0, 1), (-1, -1), (-1, 1), (1, -1), (1, 1)]
NT = (((1,), (1,)), ((), ()))


def iota(shape, axis):
    return lax.broadcasted_iota(jnp.int32, shape, axis)


def kernel(
    size_gx,
    size_gy,
    size_gz,
    capacity,
    block_rows,
    *refs,
):
    sources, out = refs[:11], refs[11]
    (feat, slot, weight, bias, owner, edge, w_in, b_in, w_mid, b_mid, w_out) = refs[12:23]
    (
        plain,
        ext,
        taps,
        pick,
        placing,
        conv,
        bins_at,
        pooled,
        z_send,
        z_left,
        z_right,
        rows_send,
        rows_recv,
        ids_send,
        ids_recv,
        scores,
        scores_recv,
        w_sem,
        xy_ssem,
        xy_rsem,
        z_ssem,
        z_rsem,
        row_ssem,
        row_rsem,
        id_ssem,
        id_rsem,
        sc_ssem,
        sc_rsem,
    ) = refs[23:]
    groups = size_gx * size_gy
    channels, bx, by, bz = feat.shape
    gx, gy, gz = lax.axis_index("gx"), lax.axis_index("gy"), lax.axis_index("gz")
    me = gx * size_gy + gy
    pairs = by // 2

    loads = [
        pltpu.make_async_copy(source, refs[12 + i], w_sem.at[i]) for i, source in enumerate(sources)
    ]
    loads[0].start()

    ext[0] = jnp.zeros(ext.shape[1:], BF)
    ext[bx + 1] = jnp.zeros(ext.shape[1:], BF)
    for x in range(bx):
        ext[x + 1, 0] = jnp.zeros(ext.shape[2:], BF)
        ext[x + 1, by + 1] = jnp.zeros(ext.shape[2:], BF)
    z_left[...] = jnp.zeros_like(z_left)
    z_right[...] = jnp.zeros_like(z_right)
    if block_rows < LANES:
        spare = (groups, LANES - block_rows, LANES)
        rows_recv[:, block_rows:] = jnp.zeros(spare, BF)

    peers = [lax.rem(me + k, groups) for k in range(groups)]
    peer_ids = [{"gx": p // size_gy, "gy": lax.rem(p, size_gy)} for p in peers]
    has_left, has_right = gz > 0, gz < size_gz - 1
    barrier = pltpu.get_barrier_semaphore()
    for k in range(1, groups):
        pl.semaphore_signal(barrier, inc=1, device_id=peer_ids[k], device_id_type=MESH)

    @pl.when(has_left)
    def _():
        pl.semaphore_signal(barrier, inc=1, device_id={"gz": gz - 1}, device_id_type=MESH)

    @pl.when(has_right)
    def _():
        pl.semaphore_signal(barrier, inc=1, device_id={"gz": gz + 1}, device_id_type=MESH)

    for load in loads[1:]:
        load.start()

    loads[0].wait()
    plain[...] = feat[...].astype(F32).reshape(plain.shape)
    for x in range(bx):
        for y in range(by):
            part = plain[pl.ds(x * by + y, channels, stride=bx * by), :]
            ext[x + 1, y + 1] = part.astype(BF)

    greeted = groups - 1 + jnp.minimum(gz, 1) + jnp.minimum(size_gz - 1 - gz, 1)
    pl.semaphore_wait(barrier, greeted)

    def span(side, length):
        if side == 0:
            return pl.ds(1, length), pl.ds(1, length)
        return (pl.ds(length, 1), pl.ds(0, 1)) if side > 0 else (pl.ds(1, 1), pl.ds(length + 1, 1))

    def exists(sx, sy):
        x, y = gx + sx, gy + sy
        return (x >= 0) & (x < size_gx) & (y >= 0) & (y < size_gy)

    xy_copies = []
    for i, (sx, sy) in enumerate(SIDES):
        (x_from, x_to), (y_from, y_to) = span(sx, bx), span(sy, by)
        xy_copies.append(
            pltpu.make_async_remote_copy(
                src_ref=ext.at[x_from, y_from],
                dst_ref=ext.at[x_to, y_to],
                send_sem=xy_ssem.at[i],
                recv_sem=xy_rsem.at[i],
                device_id={"gx": gx + sx, "gy": gy + sy},
                device_id_type=MESH,
            )
        )
        pl.when(exists(sx, sy))(xy_copies[i].start)

    for load in loads[1:6]:
        load.wait()

    owner_row = owner[...]
    edge_row = edge[...]
    marks = iota((groups, LANES), 0) == owner_row
    marks_f = marks.astype(F32)
    before = (iota((LANES, LANES), 0) < iota((LANES, LANES), 1)).astype(BF)
    earlier = jnp.dot(marks_f.astype(BF), before, preferred_element_type=F32)
    rank = jnp.sum(earlier * marks_f, axis=0, keepdims=True).astype(jnp.int32)
    row_at = iota((LANES, LANES), 0)
    slot_marks = ((row_at == rank) | (row_at == rank + capacity)).astype(F32).astype(BF)
    numbered = jnp.where(marks, (edge_row + 1).astype(F32), 0.0).astype(BF)
    ids = lax.dot_general(numbered, slot_marks, NT, preferred_element_type=F32)
    ids = ids.astype(jnp.int32) - 1
    for g in range(groups):
        ids_send[g] = jnp.broadcast_to(ids[g : g + 1], (8, LANES))
    id_copies, row_copies, score_copies = [], [], []
    for k in range(1, groups):
        id_copies.append(
            pltpu.make_async_remote_copy(
                src_ref=ids_send.at[peers[k]],
                dst_ref=ids_recv.at[me],
                send_sem=id_ssem.at[k],
                recv_sem=id_rsem.at[k],
                device_id=peer_ids[k],
                device_id_type=MESH,
            )
        )
        row_copies.append(
            pltpu.make_async_remote_copy(
                src_ref=rows_send.at[peers[k]],
                dst_ref=rows_recv.at[me, pl.ds(0, block_rows)],
                send_sem=row_ssem.at[k],
                recv_sem=row_rsem.at[k],
                device_id=peer_ids[k],
                device_id_type=MESH,
            )
        )
        score_copies.append(
            pltpu.make_async_remote_copy(
                src_ref=scores,
                dst_ref=scores_recv.at[me],
                send_sem=sc_ssem.at[k],
                recv_sem=sc_rsem.at[k],
                device_id=peer_ids[k],
                device_id_type=MESH,
            )
        )
    for copy in id_copies:
        copy.start()
    ids_recv[me] = ids_send[me]

    width = 4 * channels
    spread = iota((channels, width), 1) == iota((channels, width), 0)
    placed = jnp.dot(
        weight[...].reshape(27 * channels, channels),
        spread.astype(F32).astype(BF),
        preferred_element_type=F32,
    )
    for x in range(2):
        for dz in range(3):
            row = (dz * 2 + x) * 2 * channels
            lost = 3 * (1 - x) * width
            taps[row : row + 2 * channels, lost : lost + width] = jnp.zeros((2 * channels, width), BF)
    for dz in range(3):
        for dx in range(3):
            block = None
            for dy in range(3):
                tap = 9 * dx + 3 * dy + dz
                term = placed[tap * channels : (tap + 1) * channels]
                term = pltpu.roll(term, dy * channels, 1) if dy else term
                block = term if block is None else block + term
            both = jnp.concatenate([block, pltpu.roll(block, channels, 1)], axis=0).astype(BF)
            for x in range(2):
                row = (dz * 2 + x) * 2 * channels
                taps[row : row + 2 * channels, (x + dx) * width : (x + dx + 1) * width] = both

    at_z, lane = iota((bz, LANES), 0), iota((bz, LANES), 1)
    last_z, first_z = at_z == bz - 1, at_z == 0
    for y in range(by + 2):
        chosen_z = (last_z & (lane == y)) | (first_z & (lane == y + 64))
        pick[y * bz : (y + 1) * bz] = chosen_z.astype(F32).astype(BF)

    target = owner_row * block_rows + rank
    block_at = iota((block_rows, LANES), 0)
    for g in range(groups):
        at = block_at + g * block_rows
        mine = owner_row == g
        placing[0, g * block_rows : (g + 1) * block_rows] = (
            ((at == target) & mine).astype(F32).astype(BF)
        )
        placing[1, g * block_rows : (g + 1) * block_rows] = (
            ((at == target + capacity) & mine).astype(F32).astype(BF)
        )

    def mark_bins(j, carry):
        for part in range(4):
            x, y = part // 2, part % 2
            line = slot[pl.ds(x * by + 2 * j + y, 1), :] & (LANES - 1)
            hot = iota((LANES, bz), 0) == line
            bins_at[j, :, part * bz : (part + 1) * bz] = hot.astype(F32).astype(BF)
        return carry

    lax.fori_loop(0, pairs, mark_bins, 0)

    for i, (sx, sy) in enumerate(SIDES):
        pl.when(exists(-sx, -sy))(xy_copies[i].wait_recv)

    cut = jnp.concatenate(
        [ext[:, y].reshape((bx + 2) * channels, bz) for y in range(by + 2)], axis=1
    )
    z_send[...] = jnp.dot(cut, pick[...], preferred_element_type=F32).astype(BF)
    to_right = pltpu.make_async_remote_copy(
        src_ref=z_send,
        dst_ref=z_left,
        send_sem=z_ssem.at[0],
        recv_sem=z_rsem.at[0],
        device_id={"gz": gz + 1},
        device_id_type=MESH,
    )
    to_left = pltpu.make_async_remote_copy(
        src_ref=z_send,
        dst_ref=z_right,
        send_sem=z_ssem.at[1],
        recv_sem=z_rsem.at[1],
        device_id={"gz": gz - 1},
        device_id_type=MESH,
    )
    pl.when(has_right)(to_right.start)
    pl.when(has_left)(to_left.start)

    def convolve(i, carry):
        window = jnp.concatenate(
            [
                ext[:, pl.ds(4 * i + 2 * half, 4)].reshape((bx + 2) * 4 * channels, bz)
                for half in range(2)
            ],
            axis=1,
        )
        result = jnp.dot(taps[...], window, preferred_element_type=F32)
        conv[2 * i] = result[:, :bz]
        conv[2 * i + 1] = result[:, bz:]
        return carry

    lax.fori_loop(0, pairs // 2, convolve, 0)

    pl.when(has_left)(to_right.wait_recv)
    pl.when(has_right)(to_left.wait_recv)
    zlane = iota(z_left.shape, 1)
    faces = jnp.where(zlane < 64, z_left[...].astype(F32), z_right[...].astype(F32))
    moved = [faces] + [pltpu.roll(faces, LANES - y, 1) for y in range(1, 4)]
    window = jnp.concatenate(
        [
            moved[y][x * channels : (x + 1) * channels]
            for x in range(bx + 2)
            for y in range(4)
        ],
        axis=0,
    ).astype(BF)
    ends = jnp.dot(taps[...], window, preferred_element_type=F32)
    mrows = 4 * channels

    pooled[...] = jnp.zeros_like(pooled)
    lane32 = iota((channels, bz), 1)
    own_channel = iota((channels, channels), 0) == iota((channels, channels), 1)
    bias_col = jnp.sum(jnp.where(own_channel, bias[...], 0.0), axis=1, keepdims=True)

    def pool(j, carry):
        wide = []
        for part in range(4):
            x, y = part // 2, part % 2
            row = part * channels
            base = (x * 2) * channels
            height = 2 * j + y
            low = pltpu.roll(ends[base : base + channels], LANES - height, 1)
            high = pltpu.roll(ends[2 * mrows + base : 2 * mrows + base + channels], 63 - height, 1)
            lower = pltpu.roll(conv[j, row : row + channels], 1, 1)
            upper = pltpu.roll(conv[j, 2 * mrows + row : 2 * mrows + row + channels], bz - 1, 1)
            total = conv[j, mrows + row : mrows + row + channels]
            total = total + jnp.where(lane32 == 0, low, lower)
            total = total + jnp.where(lane32 == bz - 1, high, upper)
            field = jnp.maximum(total + bias_col, 0.0)
            bin_row = slot[pl.ds(x * by + height, 1), :] >> 7
            wide.append(
                jnp.concatenate(
                    [jnp.where(bin_row == b, field, 0.0) for b in range(BINS)], axis=0
                ).astype(BF)
            )
        pooled[...] += lax.dot_general(
            bins_at[j], jnp.concatenate(wide, axis=1), NT, preferred_element_type=F32
        )
        return carry

    lax.fori_loop(0, pairs, pool, 0, unroll=4)
    share = (LANES * BINS) / (bx * by * bz)
    rows = (pooled[...] * share).astype(BF)

    sent = jnp.dot(placing[0], rows[:, :LANES], preferred_element_type=F32) + jnp.dot(
        placing[1], rows[:, LANES:], preferred_element_type=F32
    )
    rows_send[...] = sent.astype(BF).reshape(rows_send.shape)
    for copy in row_copies:
        copy.start()
    rows_recv[me, 0:block_rows] = rows_send[me]

    for copy in id_copies:
        copy.wait_recv()
    at_lane = iota((EDGE_DEV, LANES), 1)
    at_edge = iota((EDGE_DEV, LANES), 0)
    first_half, second_half = [], []
    for g in range(groups):
        named = ids_recv[g][0:1] == at_edge
        first_half.append((named & (at_lane < capacity)).astype(F32).astype(BF))
        second_half.append(
            (named & (at_lane >= capacity) & (at_lane < 2 * capacity)).astype(F32).astype(BF)
        )
    first_half = jnp.concatenate(first_half, axis=1)
    second_half = jnp.concatenate(second_half, axis=1)
    for load in loads[6:]:
        load.wait()
    for copy in row_copies:
        copy.wait_recv()
    arrived = rows_recv[...].reshape(groups * LANES, LANES)
    edge_rows = jnp.concatenate(
        [
            jnp.dot(first_half, arrived, preferred_element_type=F32),
            jnp.dot(second_half, arrived, preferred_element_type=F32),
        ],
        axis=1,
    ).astype(BF)

    def silu(v):
        return v / (1.0 + jnp.exp(-v))

    first = silu(jnp.dot(edge_rows, w_in[...], preferred_element_type=F32) + b_in[...]).astype(BF)
    second = silu(jnp.dot(first, w_mid[...], preferred_element_type=F32) + b_mid[...]).astype(BF)
    last = jnp.broadcast_to(w_out[...].astype(F32).reshape(1, -1), (16, w_out.shape[0])).astype(BF)
    final = lax.dot_general(last, second, NT, preferred_element_type=F32)
    scores[...] = jnp.concatenate([final[:8], final[8:]], axis=1)
    for copy in score_copies:
        copy.start()
    scores_recv[me] = scores[...]
    edge_hot = (iota((LANES, LANES), 0) == edge_row).astype(F32)
    for copy in score_copies:
        copy.wait_recv()
    table = jnp.concatenate([scores_recv[g][0:1] for g in range(groups)], axis=0)
    chosen = jnp.dot(table, edge_hot, preferred_element_type=F32, precision=lax.Precision.HIGHEST)
    out[...] = jnp.sum(jnp.where(marks, chosen, 0.0), axis=0, keepdims=True)

    for i, (sx, sy) in enumerate(SIDES):
        pl.when(exists(sx, sy))(xy_copies[i].wait_send)
    pl.when(has_right)(to_right.wait_send)
    pl.when(has_left)(to_left.wait_send)
    for copy in id_copies + row_copies + score_copies:
        copy.wait_send()


def body(
    features,
    voxel_slot,
    conv_weight,
    conv_bias,
    pair_owner,
    pair_edge,
    mlp_in,
    mlp_in_bias,
    mlp_mid,
    mlp_mid_bias,
    mlp_out,
):
    channels, bx, by, bz = features.shape
    sizes = [lax.axis_size(axis) for axis in ("gx", "gy", "gz")]
    groups = sizes[0] * sizes[1]
    pair_count = pair_edge.shape[0]
    capacity = max(2, (5 * pair_count + 2 * groups - 1) // (2 * groups))
    block_rows = -(-2 * capacity // 16) * 16
    hidden = mlp_mid.shape[0]
    vmem = pl.BlockSpec(memory_space=pltpu.VMEM)
    hbm = pl.BlockSpec(memory_space=pltpu.HBM)
    operands = (
        features,
        voxel_slot.reshape(bx * by, bz),
        conv_weight,
        conv_bias.reshape(1, channels),
        pair_owner.reshape(1, pair_count),
        pair_edge.reshape(1, pair_count),
        mlp_in,
        mlp_in_bias.reshape(1, hidden),
        mlp_mid,
        mlp_mid_bias.reshape(1, hidden),
        mlp_out,
    )
    sems = pltpu.SemaphoreType.DMA
    result = pl.pallas_call(
        functools.partial(kernel, *sizes, capacity, block_rows),
        out_shape=jax.ShapeDtypeStruct((1, pair_count), F32),
        in_specs=[hbm] * len(operands),
        out_specs=vmem,
        scratch_shapes=[pltpu.VMEM(a.shape, a.dtype) for a in operands]
        + [
            pltpu.VMEM((channels * bx * by, bz), F32),
            pltpu.VMEM((bx + 2, by + 2, channels, bz), BF),
            pltpu.VMEM((12 * channels, 16 * channels), BF),
            pltpu.VMEM(((by + 2) * bz, LANES), BF),
            pltpu.VMEM((2, groups * block_rows, LANES), BF),
            pltpu.VMEM((by // 2, 12 * channels, bz), F32),
            pltpu.VMEM((by // 2, LANES, 4 * bz), BF),
            pltpu.VMEM((pair_count, BINS * channels), F32),
            pltpu.VMEM(((bx + 2) * channels, LANES), BF),
            pltpu.VMEM(((bx + 2) * channels, LANES), BF),
            pltpu.VMEM(((bx + 2) * channels, LANES), BF),
            pltpu.VMEM((groups, block_rows, LANES), BF),
            pltpu.VMEM((groups, LANES, LANES), BF),
            pltpu.VMEM((groups, 8, LANES), jnp.int32),
            pltpu.VMEM((groups, 8, LANES), jnp.int32),
            pltpu.VMEM((8, LANES), F32),
            pltpu.VMEM((groups, 8, LANES), F32),
            sems((len(operands),)),
            sems((8,)),
            sems((8,)),
            sems((2,)),
            sems((2,)),
            sems((groups,)),
            sems((groups,)),
            sems((groups,)),
            sems((groups,)),
            sems((groups,)),
            sems((groups,)),
        ],
        compiler_params=pltpu.CompilerParams(
            collective_id=0, has_side_effects=True, vmem_limit_bytes=63 * 2**20
        ),
    )(*operands)
    return result.reshape(pair_count)


def solution(mesh):
    placed = (
        P(None, "gx", "gy", "gz"),
        P("gx", "gy", "gz"),
        P(),
        P(),
        P(("gx", "gy", "gz"), None),
        P(("gx", "gy", "gz")),
        P(),
        P(),
        P(),
        P(),
        P(),
    )
    return jax.shard_map(
        body, mesh=mesh, in_specs=placed, out_specs=P(("gx", "gy", "gz")), check_vma=False
    )
```
